256 devices in a mesh: enc: 4 (over z_hi, core), dec: 4 (over z_lo), dp: 16 (over x, y).
Axes of the slice: x: 4, y: 4, z: 8 (z_hi: 2, z_lo: 4; z = z_hi * 4 + z_lo), core: 2. Of those that a mesh axis runs over, the one named last changes fastest.
Arguments:
- src_embed: bfloat16 [4, 128, 4096], P('dec'), may hold values from -8 to 8
- tgt_embed: bfloat16 [4, 128, 4096], P('enc'), may hold values from -8 to 8
- src_lengths: int32 [4], replicated, may hold values from 32 to 128
- enc_gain: float32 [4, 4096], P('enc'), may hold values from 0.1 to 1.9
- enc_project: bfloat16 [4, 4096, 3, 4096], P('enc', 'dec', None, 'dp'), may hold values from -0.09375 to 0.09375
- enc_output: bfloat16 [4, 4096, 4096], P('enc', 'dp', 'dec'), may hold values from -0.09375 to 0.09375
- final_gain: float32 [4096], replicated, may hold values from 0.1 to 1.9
- dec_gain: float32 [4, 4096], P('dec'), may hold values from 0.3 to 3
- dec_query: bfloat16 [4, 4096, 4096], P('dec', 'enc', 'dp'), may hold values from -0.09375 to 0.09375
- dec_memory: bfloat16 [4, 4096, 2, 4096], P('dec', 'enc', None, 'dp'), may hold values from -0.09375 to 0.09375
- dec_output: bfloat16 [4, 4096, 4096], P('dec', 'dp', 'enc'), may hold values from -0.09375 to 0.09375
Outputs:
- enc_states: bfloat16 [4, 4, 128, 4096], P('enc', 'dec')
- dec_states: bfloat16 [4, 4, 128, 4096], P('dec', 'enc')
The draws below stay inside these ranges and needn't reach their ends.
All inputs are finite; a program needn't handle non-finite values.
Results may differ from the reference program's by a relative error of at most 0.035.
Values may be sent and summed in bfloat16 or wider, within the bound.
No kernel may reach another device: no remote copies, remote signals or barrier semaphores. Data moves between devices by JAX's collectives and lax.ppermute only.
A program may use at most 64 MiB of HBM per device.

```python
import math
import jax
import jax.numpy as jnp
from jax import lax

D = 4096
HEADS = 16
HD = 256
SRC = 128
TGT = 128
ENC_LAYERS = 4
DEC_LAYERS = 4
MICRO = 4
N_DP = 16


def feature_signs(key):
    coin_flips = jax.random.bernoulli(jax.random.fold_in(key, 101), 0.5, (D,))
    return jnp.where(coin_flips, 1.0, -1.0).astype(jnp.float32)


def column_signs(key, salt_value, layer_count):
    coin_flips = jax.random.bernoulli(jax.random.fold_in(key, salt_value), 0.5, (layer_count, HEADS * HD))
    return jnp.where(coin_flips, 1.0, -1.0).astype(jnp.float32)


def draw_src_embed(key, part):
    features = feature_signs(key)
    key = jax.random.fold_in(key, 1)
    extent = (MICRO, SRC, D)
    gauss_draw = jnp.clip(jax.random.normal(key, extent, jnp.float32), -6.0, 6.0)
    return (gauss_draw * features).astype(jnp.bfloat16)


def draw_tgt_embed(key, part):
    features = feature_signs(key)
    key = jax.random.fold_in(key, 2)
    extent = (MICRO, TGT, D)
    gauss_draw = jnp.clip(jax.random.normal(key, extent, jnp.float32), -6.0, 6.0)
    return (gauss_draw * features).astype(jnp.bfloat16)


def draw_enc_project(key, part):
    features = feature_signs(key)
    columns = column_signs(key, 303, ENC_LAYERS)
    key = jax.random.fold_in(key, 3)
    extent = (ENC_LAYERS, D, 3, HEADS * HD)
    gauss_draw = jnp.clip(jax.random.normal(key, extent, jnp.float32), -6.0, 6.0) * D ** (-0.5)
    return (gauss_draw * features[None, :, None, None] * columns[:, None, None, :]).astype(jnp.bfloat16)


def draw_dec_query(key, part):
    features = feature_signs(key)
    columns = column_signs(key, 404, DEC_LAYERS)
    key = jax.random.fold_in(key, 5)
    extent = (DEC_LAYERS, D, HEADS * HD)
    gauss_draw = jnp.clip(jax.random.normal(key, extent, jnp.float32), -6.0, 6.0) * D ** (-0.5)
    return (gauss_draw * features[None, :, None] * columns[:, None, :]).astype(jnp.bfloat16)


def draw_dec_memory(key, part):
    features = feature_signs(key)
    columns = column_signs(key, 404, DEC_LAYERS)
    key = jax.random.fold_in(key, 7)
    extent = (DEC_LAYERS, D, 2, HEADS * HD)
    gauss_draw = jnp.clip(jax.random.normal(key, extent, jnp.float32), -6.0, 6.0) * D ** (-0.5)
    return (gauss_draw * features[None, :, None, None] * columns[:, None, None, :]).astype(jnp.bfloat16)


def set_ends(values, key, least, largest):
    dims = values.shape
    index_at = [jax.random.randint(jax.random.fold_in(key, axis), (), 0, dims[axis]) for axis in range(len(dims))]
    values = values.at[tuple(index_at)].set(least)
    longest = dims.index(max(dims))
    index_at[longest] = (index_at[longest] + 1) % dims[longest]
    return values.at[tuple(index_at)].set(largest)


def shard_levels(key, shape, cuts, low, top_value):
    level = 1.0
    for position, blocks in cuts:
        steps = jax.random.uniform(jax.random.fold_in(jax.random.fold_in(key, 6), position), (blocks,), jnp.float32, low / len(cuts), top_value / len(cuts))
        level = level * jnp.repeat(jnp.exp(steps), shape[position] // blocks).reshape((-1,) + (1,) * (len(shape) - 1 - position))
    return level


def gaussian(rng, dims, scale, most, cuts=(), kind=jnp.bfloat16):
    values = scale * jax.random.normal(rng, dims, jnp.float32)
    if cuts:
        values = values * shard_levels(rng, dims, cuts, -0.22, 0.18)
    return jnp.clip(values, -most, most).astype(kind)


def setup_inputs(seed: int = 0) -> dict:
    key_of = jax.random.split(jax.random.key(seed), 12)
    src_embed = draw_src_embed(jax.random.fold_in(key_of[11], 71), 0)
    tgt_embed = draw_tgt_embed(jax.random.fold_in(key_of[11], 71), 0)
    src_lengths = set_ends(jax.random.randint(key_of[2], (MICRO,), SRC // 4, SRC + 1), jax.random.fold_in(key_of[2], 1), SRC // 4, SRC).astype(jnp.int32)
    enc_gain = jnp.clip(1.0 + 0.18 * jax.random.normal(key_of[3], (ENC_LAYERS, D), jnp.float32), 0.1, 1.9)
    enc_project = draw_enc_project(jax.random.fold_in(key_of[11], 71), 0)
    enc_output = gaussian(key_of[5], (ENC_LAYERS, HEADS * HD, D), (HEADS * HD) ** -0.5, 0.09375, ((0, 4), (1, 16), (2, 4)))
    final_gain = jnp.clip(1.0 + 0.18 * jax.random.normal(key_of[6], (D,), jnp.float32), 0.1, 1.9)
    dec_gain = jnp.clip(jnp.exp(math.log(3.0) - 2.3025851 * jax.random.uniform(key_of[7], (DEC_LAYERS, D), jnp.float32) ** shard_levels(key_of[7], (DEC_LAYERS, D), ((0, 4),), -0.2, 0.2)), 0.3, 3.0)
    dec_query = draw_dec_query(jax.random.fold_in(key_of[11], 71), 0)
    dec_memory = draw_dec_memory(jax.random.fold_in(key_of[11], 71), 0)
    dec_output = gaussian(key_of[10], (DEC_LAYERS, HEADS * HD, D), (HEADS * HD) ** -0.5, 0.09375, ((0, 4), (1, 16), (2, 4)))
    return dict(src_embed=src_embed, tgt_embed=tgt_embed, src_lengths=src_lengths, enc_gain=enc_gain, enc_project=enc_project, enc_output=enc_output, final_gain=final_gain, dec_gain=dec_gain, dec_query=dec_query, dec_memory=dec_memory, dec_output=dec_output)


def normalize(values, gain):
    wide = values.astype(jnp.float32)
    return wide * lax.rsqrt(lax.optimization_barrier(jnp.mean(wide * wide, axis=-1, keepdims=True)) + 1e-06) * gain

def attend(query, keys, values, length):
    rows = query.shape[0]
    span = keys.shape[0]
    query_heads = query.reshape(rows, -1, HD).astype(jnp.float32)
    key_heads = keys.reshape(span, -1, HD).astype(jnp.float32)
    value_heads = values.reshape(span, -1, HD).astype(jnp.float32)
    scores = jnp.einsum('rhc,shc->hrs', query_heads, key_heads) * (1.0 / math.sqrt(HD))
    valid = jnp.arange(span) < length
    scores = jnp.where(valid[None, None, :], scores, -1e+30)
    top = lax.optimization_barrier(jnp.max(scores, axis=-1, keepdims=True))
    weights = jnp.exp(scores - top)
    weights = weights / lax.optimization_barrier(jnp.sum(weights, axis=-1, keepdims=True))
    probs = lax.optimization_barrier(weights.astype(jnp.bfloat16)).astype(jnp.float32)
    mixed = jnp.einsum('hrs,shc->rhc', probs, value_heads)
    return mixed.astype(jnp.bfloat16).reshape(rows, -1)

def project_out(attended, weight):
    rows = attended.shape[0]
    width = weight.shape[1]
    grouped = attended.reshape(rows, N_DP, -1).astype(jnp.float32)
    blocks = weight.reshape(N_DP, -1, width).astype(jnp.float32)
    terms = jnp.einsum('rgc,gcd->rgd', grouped, blocks)
    terms = lax.optimization_barrier(terms.astype(jnp.bfloat16)).astype(jnp.float32)
    return lax.optimization_barrier(jnp.sum(terms, axis=1))

def layer(current, gain, weight_in, weight_out, length, memory_pair):
    normed = normalize(current, gain).astype(jnp.bfloat16)
    count = weight_in.shape[1]
    mixed = jnp.dot(normed, weight_in.reshape(D, -1), preferred_element_type=jnp.float32)
    mixed = mixed.astype(jnp.bfloat16).reshape(current.shape[0], count, -1)
    if memory_pair is None:
        query, keys, values = (mixed[:, 0], mixed[:, 1], mixed[:, 2])
    else:
        query = mixed[:, 0]
        keys, values = memory_pair
    attended = attend(query, keys, values, length)
    return (current.astype(jnp.float32) + project_out(attended, weight_out)).astype(jnp.bfloat16)

def reference(src_embed, tgt_embed, src_lengths, enc_gain, enc_project, enc_output, final_gain, dec_gain, dec_query, dec_memory, dec_output):
    encoder_rows = []
    memories = []
    for batch in range(MICRO):
        current = src_embed[batch]
        stacked = []
        for level in range(ENC_LAYERS):
            current = layer(current, enc_gain[level], enc_project[level], enc_output[level], src_lengths[batch], None)
            stacked.append(current)
        encoder_rows.append(jnp.stack(stacked))
        memories.append(normalize(current, final_gain).astype(jnp.bfloat16))
    enc_states = jnp.stack(encoder_rows, axis=1)
    decoder_rows = []
    for batch in range(MICRO):
        current = tgt_embed[batch]
        stacked = []
        for level in range(DEC_LAYERS):
            pairs = jnp.dot(memories[batch], dec_memory[level].reshape(D, -1), preferred_element_type=jnp.float32)
            pairs = pairs.astype(jnp.bfloat16).reshape(SRC, 2, -1)
            current = layer(current, dec_gain[level], dec_query[level][:, None, :], dec_output[level], src_lengths[batch], (pairs[:, 0], pairs[:, 1]))
            stacked.append(current)
        decoder_rows.append(jnp.stack(stacked))
    dec_states = jnp.stack(decoder_rows, axis=1)
    return (enc_states, dec_states)
```

```python
import math

import jax
import jax.numpy as jnp
from jax import lax
from jax.sharding import PartitionSpec as P

HD = 256
AXES = ("enc", "dec", "dp")


def normalize(values, gain):
    wide = values.astype(jnp.float32)
    return wide * lax.rsqrt(jnp.mean(wide * wide, axis=-1, keepdims=True) + 1e-06) * gain


def attend(query, keys, values, length):
    span = keys.shape[0]
    scores = lax.dot_general(
        query, keys, (((1,), (1,)), ((), ())), preferred_element_type=jnp.float32
    ) * (1.0 / math.sqrt(HD))
    valid = jnp.arange(span) < length
    scores = jnp.where(valid[None, :], scores, -1e30)
    top = jnp.max(scores, axis=-1, keepdims=True)
    weights = jnp.exp(scores - top)
    probs = (weights / jnp.sum(weights, axis=-1, keepdims=True)).astype(jnp.bfloat16)
    return jnp.dot(probs, values, preferred_element_type=jnp.float32).astype(jnp.bfloat16)


def pick_length(table, position):
    return jnp.sum(jnp.where(jnp.arange(table.shape[0]) == position, table, 0))


def project_rows(piece, weight):
    return jnp.einsum("rd,dkc->rkc", piece, weight, preferred_element_type=jnp.float32).astype(
        jnp.bfloat16
    )


def gather_rows(piece):
    count = lax.axis_size("dp")
    copies = jnp.broadcast_to(piece[None], (count,) + piece.shape)
    return lax.all_to_all(copies, "dp", 0, 0).reshape(-1, piece.shape[-1])


def scatter_sum(partial_sum):
    count = lax.axis_size("dp")
    blocks = partial_sum.reshape(count, -1, partial_sum.shape[-1])
    return jnp.sum(lax.all_to_all(blocks, "dp", 0, 0).astype(jnp.float32), axis=0)


def own_rows(full):
    rows = full.shape[0] // lax.axis_size("dp")
    return lax.dynamic_slice_in_dim(full, lax.axis_index("dp") * rows, rows, 0)


def on_device(
    src_embed,
    tgt_embed,
    src_lengths,
    enc_gain,
    enc_project,
    enc_output,
    final_gain,
    dec_gain,
    dec_query,
    dec_memory,
    dec_output,
):
    sections_enc = lax.axis_size("enc")
    sections_dec = lax.axis_size("dec")
    enc_place = lax.axis_index("enc")
    dec_place = lax.axis_index("dec")
    enc_length = pick_length(src_lengths, dec_place)
    dec_length = pick_length(src_lengths, enc_place)
    enc_weight_in = lax.all_gather(enc_project[0], "dec", axis=0, tiled=True)
    enc_weight_out = lax.all_gather(enc_output[0], "dec", axis=1, tiled=True)
    dec_weight_memory = lax.all_gather(dec_memory[0], "enc", axis=0, tiled=True)
    dec_weight_query = lax.all_gather(dec_query[0], "enc", axis=0, tiled=True)
    dec_weight_out = lax.all_gather(dec_output[0], "enc", axis=1, tiled=True)

    current = src_embed[0]
    piece = own_rows(current)
    enc_piece = piece
    for step in range(sections_enc):
        normed = normalize(current, enc_gain[0]).astype(jnp.bfloat16)
        mixed = project_rows(normed, enc_weight_in)
        attended = attend(mixed[:, 0], mixed[:, 1], mixed[:, 2], enc_length)
        partial_sum = jnp.dot(attended, enc_weight_out, preferred_element_type=jnp.float32)
        summed = scatter_sum(partial_sum.astype(jnp.bfloat16))
        result = (piece.astype(jnp.float32) + summed).astype(jnp.bfloat16)
        enc_piece = jnp.where(enc_place == step, result, enc_piece)
        if step + 1 < sections_enc:
            piece = lax.ppermute(result, "enc", [(step, step + 1)])
            current = gather_rows(piece)

    memory_piece = normalize(enc_piece, final_gain).astype(jnp.bfloat16)
    parts = lax.axis_size("dp")
    last = sections_enc - 1

    def place(e, d, p):
        return (e * sections_dec + d) * parts + p

    memory_here = jnp.zeros_like(memory_piece)
    for by in range(sections_dec):
        pairs = [
            (place(last, m, p), place(m, (m + by) % sections_dec, p))
            for m in range(sections_dec)
            for p in range(parts)
        ]
        pairs_moved = [(a, b) for a, b in pairs if a != b]
        memory_here = memory_here + lax.ppermute(memory_piece, AXES, pairs_moved)
    stays = (enc_place == last) & (dec_place == last)
    memory_here = jnp.where(stays, memory_piece, memory_here)
    memory = gather_rows(memory_here)
    pairs = project_rows(memory, dec_weight_memory)
    keys, values = pairs[:, 0], pairs[:, 1]

    current = tgt_embed[0]
    piece = own_rows(current)
    dec_piece = piece
    enc_state = lax.all_gather(enc_piece, "dp", axis=0, tiled=True)
    for step in range(sections_dec):
        if step == sections_dec - 1:
            current, enc_state = lax.optimization_barrier((current, enc_state))
        normed = normalize(current, dec_gain[0]).astype(jnp.bfloat16)
        query = jnp.dot(normed, dec_weight_query, preferred_element_type=jnp.float32)
        attended = attend(query.astype(jnp.bfloat16), keys, values, dec_length)
        partial_sum = jnp.dot(attended, dec_weight_out, preferred_element_type=jnp.float32)
        summed = scatter_sum(partial_sum.astype(jnp.bfloat16))
        result = (piece.astype(jnp.float32) + summed).astype(jnp.bfloat16)
        dec_piece = jnp.where(dec_place == step, result, dec_piece)
        if step + 1 < sections_dec:
            piece = lax.ppermute(result, "dec", [(step, step + 1)])
            current = gather_rows(piece)
    dec_state = gather_rows(dec_piece)
    return (enc_state[None, None], dec_state[None, None])


def solution(mesh):
    placed = (
        P("dec", None, None),
        P("enc", None, None),
        P(),
        P("enc", None),
        P("enc", "dec", None, "dp"),
        P("enc", "dp", "dec"),
        P(),
        P("dec", None),
        P("dec", "enc", "dp"),
        P("dec", "enc", None, "dp"),
        P("dec", "dp", "enc"),
    )
    return jax.shard_map(
        on_device,
        mesh=mesh,
        in_specs=placed,
        out_specs=(P("enc", "dec", None, None), P("dec", "enc", None, None)),
        check_vma=False,
    )
```

```python
import math

import jax
import jax.numpy as jnp
from jax import lax
from jax.sharding import PartitionSpec as P

HD = 256


def normalize(values, gain):
    wide = values.astype(jnp.float32)
    return wide * lax.rsqrt(jnp.mean(wide * wide, axis=-1, keepdims=True) + 1e-06) * gain


def attend(query, keys, values, positions, length):
    scores = lax.dot_general(
        query, keys, (((1,), (1,)), ((), ())), preferred_element_type=jnp.float32
    ) * (1.0 / math.sqrt(HD))
    scores = jnp.where((positions < length)[None, :], scores, -1e30)
    top = jnp.max(scores, axis=-1, keepdims=True)
    weights = jnp.exp(scores - top)
    probs = (weights / jnp.sum(weights, axis=-1, keepdims=True)).astype(jnp.bfloat16)
    return jnp.dot(probs, values, preferred_element_type=jnp.float32).astype(jnp.bfloat16)


def pick_length(table, position):
    return jnp.sum(jnp.where(jnp.arange(table.shape[0]) == position, table, 0))


def spread(block, axis):
    copies = jnp.broadcast_to(block[None], (lax.axis_size(axis),) + block.shape)
    return lax.all_to_all(copies, axis, 0, 0)


def exchange_sum(blocks, axis):
    return jnp.sum(lax.all_to_all(blocks, axis, 0, 0).astype(jnp.float32), axis=0)


def beside(blocks, moves):
    blocks, chunks = lax.optimization_barrier((blocks, [chunk for chunk, _, _ in moves]))
    got = [lax.ppermute(c, axis, pairs) for c, (_, axis, pairs) in zip(chunks, moves)]
    return lax.optimization_barrier((lax.all_to_all(blocks, "dp", 0, 0), got))


def with_squares(terms, squares):
    coarse = squares.astype(jnp.bfloat16)
    fine = (squares - coarse.astype(jnp.float32)).astype(jnp.bfloat16)
    return jnp.concatenate([terms, jnp.where(jnp.arange(128) < 64, coarse, fine)], axis=-1)


def normalized(total, width):
    n = total.shape[-1] - 128
    mean = (total[..., n : n + 1] + total[..., n + 64 : n + 65]) / width
    return (total[..., :n] * lax.rsqrt(mean + 1e-06)).astype(jnp.bfloat16)


def add_up(blocks):
    return jnp.sum(blocks.astype(jnp.float32), axis=0)


def from_own(values, place):
    blocks = jnp.split(values, 4, axis=-1)
    near = place % 2 == 1
    far = place >= 2
    paired = [jnp.where(near, blocks[i ^ 1], blocks[i]) for i in range(4)]
    blocks = [jnp.where(far, paired[i ^ 2], paired[i]) for i in range(4)]
    return jnp.concatenate([blocks[0], blocks[2], blocks[1], blocks[3]], axis=-1)


def to_own(values, place):
    blocks = jnp.split(values, 4, axis=-1)
    blocks = [blocks[0], blocks[2], blocks[1], blocks[3]]
    near = place % 2 == 1
    far = place >= 2
    paired = [jnp.where(near, blocks[i ^ 1], blocks[i]) for i in range(4)]
    return jnp.concatenate([jnp.where(far, paired[i ^ 2], paired[i]) for i in range(4)], axis=-1)


def own_rows(full):
    rows = full.shape[0] // lax.axis_size("dp")
    return lax.dynamic_slice_in_dim(full, lax.axis_index("dp") * rows, rows, 0)


def on_device(
    src_embed,
    tgt_embed,
    src_lengths,
    enc_gain,
    enc_project,
    enc_output,
    final_gain,
    dec_gain,
    dec_query,
    dec_memory,
    dec_output,
):
    enc_place = lax.axis_index("enc")
    dec_place = lax.axis_index("dec")
    place = lax.axis_index("dp")
    n_dec = lax.axis_size("dec")
    n_dp = lax.axis_size("dp")
    core = enc_place % 2
    late = enc_place >= 2
    swap = [(0, 1), (1, 0), (2, 3), (3, 2)]
    early, later = (0, 1), (2, 3)
    enc_length = pick_length(src_lengths, dec_place)
    dec_length = pick_length(src_lengths, enc_place)

    src = src_embed[0]
    rows, width = src.shape
    half = rows // 2
    own = half // n_dp
    block = width // n_dec

    shard_memory = dec_memory[0].reshape(block, 2 * HD)

    def far(shard, places):
        pairs = [(e * n_dec + d, (e ^ 2) * n_dec + d) for e in range(4) for d in places]
        return lax.ppermute(shard, ("enc", "dec"), pairs)

    def with_near(mine, axis):
        return jnp.concatenate([mine, lax.ppermute(mine, "enc", swap)], axis=axis)

    def joined(mine, remote, axis):
        return with_near(jnp.concatenate([mine, remote], axis=axis), axis)

    def both(mine):
        other = lax.ppermute(mine, "enc", swap)
        return [jnp.where(core == which, mine, other) for which in range(2)]

    weights_in = both(enc_project[0].reshape(block, 3 * HD))
    weights_out = both(enc_output[0])
    gains = [lax.dynamic_slice_in_dim(g[0], dec_place * block, block) for g in both(enc_gain)]

    mine = lax.dynamic_slice_in_dim(src, core * half, half, 0)
    mine = mine.reshape(half, n_dec, block).transpose(1, 0, 2)
    current = lax.all_to_all(mine, "dec", 0, 0)
    piece = lax.dynamic_slice_in_dim(
        current.reshape(n_dec, n_dp, own, block), place, 1, 1
    ).reshape(n_dec * own, block)
    steps = jnp.arange(half)
    key_places = jnp.concatenate([core * half + steps, (1 - core) * half + steps])
    states = []
    for step in range(4):
        which = step % 2
        wide = current.astype(jnp.float32)
        squares = jnp.sum(wide * wide, axis=-1, keepdims=True)
        scaled = (wide * gains[which]).astype(jnp.bfloat16)
        terms = jnp.einsum(
            "mtc,cn->mtn", scaled, weights_in[which], preferred_element_type=jnp.float32
        ).astype(jnp.bfloat16)
        mixed = normalized(exchange_sum(with_squares(terms, squares), "dec"), width)
        pair = mixed[:, HD:]
        pair = jnp.concatenate([pair, lax.ppermute(pair, "enc", swap)], axis=0)
        attended = attend(mixed[:, :HD], pair[:, :HD], pair[:, HD:], key_places, enc_length)
        everyone = spread(attended, "dec").reshape(n_dec, n_dp, own, HD)
        everyone = everyone.transpose(1, 0, 2, 3).reshape(n_dec * half, HD)
        terms = jnp.dot(everyone, weights_out[which], preferred_element_type=jnp.float32)
        terms = terms.astype(jnp.bfloat16).reshape(n_dp, n_dec * own, block)
        moving = []
        if step == 0:
            terms, shard = lax.optimization_barrier((terms, dec_query[0]))
            moving = [far(shard, early), with_near(shard_memory, 0)]
        elif step == 1:
            terms, shard, far_query = lax.optimization_barrier((terms, dec_output[0], moved[0]))
            dec_weight_memory = moved[1]
            moving = [far(shard, early)]
        elif step == 2:
            terms, shard, far_out = lax.optimization_barrier((terms, dec_query[0], moved[0]))
            moving = [far(shard, later)]
        else:
            terms, got = lax.optimization_barrier((terms, moved[0]))
            far_query = jnp.where(dec_place < 2, far_query, got)
            dec_weight_query = joined(dec_query[0], far_query, 0)
        summed = exchange_sum(terms, "dp")
        piece = (piece.astype(jnp.float32) + summed).astype(jnp.bfloat16)
        states.append(piece)
        if step == 1:
            piece = lax.ppermute(piece, "enc", [(0, 2), (1, 3)])
        if step < 3:
            current = spread(piece, "dp").reshape(n_dp, n_dec, own, block)
            current, moved = lax.optimization_barrier((current, moving))
            current = current.transpose(1, 0, 2, 3).reshape(n_dec, half, block)

    def place_of(n):
        return (
            jnp.arange(n_dp)[:, None, None] * own
            + jnp.arange(2)[None, :, None] * half
            + jnp.arange(own)[None, None, :]
        ).reshape(n)

    blocks = states[3].reshape(2, 2, own, block).transpose(1, 0, 2, 3)
    blocks = jnp.broadcast_to(blocks[None, :, None], (2, 2, n_dec, 2, own, block))
    blocks = lax.all_to_all(blocks.reshape(-1, 2 * own, block), ("enc", "dec"), 0, 0)
    blocks = blocks.reshape(2, 2, 2, 2, 2, own, block)[1]
    blocks = jnp.where(late, blocks[:, 1], blocks[:, 0])
    blocks = jnp.where(core == 0, blocks, blocks[:, ::-1])
    last = blocks.transpose(2, 0, 3, 1, 4).reshape(4 * own, 2 * block)
    last, shard = lax.optimization_barrier((last, dec_output[0]))
    got = far(shard, later)
    last = spread(last, "dp")
    last, got = lax.optimization_barrier((last, got))
    far_out = jnp.where(dec_place < 2, far_out, got)
    dec_weight_out = joined(dec_output[0], far_out, 1)
    gain = jnp.concatenate(
        [
            lax.dynamic_slice_in_dim(final_gain, place * block, block)
            for place in (enc_place, enc_place + 1 - 2 * core)
        ]
    )
    wide = last.astype(jnp.float32)
    squares = jnp.sum(wide * wide, axis=-1, keepdims=True)
    scaled = (wide * gain).astype(jnp.bfloat16)
    terms = jnp.einsum(
        "hrc,cn->hrn", scaled, dec_weight_memory, preferred_element_type=jnp.float32
    )
    sent = with_squares(terms.astype(jnp.bfloat16), squares).reshape(n_dp, 2, 2 * own, -1)
    kept = jnp.where(late, sent[:, 1], sent[:, 0]).reshape(rows, -1)
    given = jnp.where(late, sent[:, 0], sent[:, 1]).reshape(rows, -1)
    total = kept.astype(jnp.float32) + far(given, range(n_dec)).astype(jnp.float32)
    pairs = normalized(total, width)
    keys, values = pairs[:, :HD], pairs[:, HD:]
    memory_places = place_of(rows)

    even = jnp.where(late, states[2], states[0])
    odd = jnp.where(late, states[3], states[1])
    kept = jnp.where(core == 0, even, odd)
    given = lax.ppermute(jnp.where(core == 0, odd, even), "enc", swap)
    halves = jnp.stack([jnp.where(core == 0, kept, given), jnp.where(core == 0, given, kept)])
    halves = halves.reshape(2, n_dec, own, block).transpose(1, 0, 2, 3)
    halves = halves.reshape(n_dec, 2 * own, block)
    moves = []
    for by in range(1, n_dec):
        along = [(i, (i + by) % n_dec) for i in range(n_dec)]
        chunk = lax.dynamic_index_in_dim(halves, (dec_place + by) % n_dec, 0, keepdims=False)
        moves.append((chunk, "dec", along))
    kept = lax.dynamic_index_in_dim(halves, dec_place, 0, keepdims=False)

    def in_order(parts):
        blocks = []
        for source in range(n_dec):
            chosen = parts[0]
            for by in range(1, n_dec):
                chosen = jnp.where((dec_place - by) % n_dec == source, parts[by], chosen)
            blocks.append(chosen)
        return jnp.concatenate(blocks, axis=-1)

    current = from_own(tgt_embed[0], enc_place)
    gain = from_own(dec_gain[0], enc_place)
    piece = own_rows(current)
    dec_piece = piece
    gathered = []
    for step in range(4):
        normed = normalize(current, gain).astype(jnp.bfloat16)
        query = jnp.dot(normed, dec_weight_query, preferred_element_type=jnp.float32)
        attended = attend(query.astype(jnp.bfloat16), keys, values, memory_places, dec_length)
        terms = jnp.dot(attended, dec_weight_out, preferred_element_type=jnp.float32)
        terms = terms.astype(jnp.bfloat16).reshape(n_dp, -1, width)
        if step == 0:
            terms, got = beside(terms, moves)
            enc_piece = in_order([kept] + got)
        elif step == 3:
            enc_state = jnp.where(dec_place == 1, gathered[1], gathered[0])
            enc_state = enc_state.reshape(n_dp, 2, own, width)
            enc_state = enc_state.transpose(1, 0, 2, 3).reshape(rows, width)
            terms, enc_state = lax.optimization_barrier((terms, enc_state))
            terms = lax.all_to_all(terms, "dp", 0, 0)
        else:
            terms = lax.all_to_all(terms, "dp", 0, 0)
        result = (piece.astype(jnp.float32) + add_up(terms)).astype(jnp.bfloat16)
        dec_piece = jnp.where(dec_place == step, result, dec_piece)
        if step < 3:
            piece = lax.ppermute(result, "dec", [(step, step + 1)])
            current = jnp.where(dec_place == step + 1, piece, enc_piece)
            current = spread(current, "dp").reshape(rows, width)
            gathered.append(current)
    dec_state = spread(to_own(dec_piece, enc_place), "dp").reshape(rows, width)
    return (enc_state[None, None], dec_state[None, None])


def solution(mesh):
    placed = (
        P("dec", None, None),
        P("enc", None, None),
        P(),
        P("enc", None),
        P("enc", "dec", None, "dp"),
        P("enc", "dp", "dec"),
        P(),
        P("dec", None),
        P("dec", "enc", "dp"),
        P("dec", "enc", None, "dp"),
        P("dec", "dp", "enc"),
    )
    return jax.shard_map(
        on_device,
        mesh=mesh,
        in_specs=placed,
        out_specs=(P("enc", "dec", None, None), P("dec", "enc", None, None)),
        check_vma=False,
    )
```

```python
import math

import jax
import jax.numpy as jnp
from jax import lax
from jax.sharding import PartitionSpec as P

HD = 256


def normalize(values, gain):
    wide = values.astype(jnp.float32)
    return wide * lax.rsqrt(jnp.mean(wide * wide, axis=-1, keepdims=True) + 1e-06) * gain


def attend(query, keys, values, positions, length):
    scores = lax.dot_general(
        query, keys, (((1,), (1,)), ((), ())), preferred_element_type=jnp.float32
    ) * (1.0 / math.sqrt(HD))
    scores = jnp.where((positions < length)[None, :], scores, -1e30)
    top = jnp.max(scores, axis=-1, keepdims=True)
    weights = jnp.exp(scores - top)
    probs = (weights / jnp.sum(weights, axis=-1, keepdims=True)).astype(jnp.bfloat16)
    return jnp.dot(probs, values, preferred_element_type=jnp.float32).astype(jnp.bfloat16)


def pick_length(table, position):
    return jnp.sum(jnp.where(jnp.arange(table.shape[0]) == position, table, 0))


def spread(block, axis):
    copies = jnp.broadcast_to(block[None], (lax.axis_size(axis),) + block.shape)
    return lax.all_to_all(copies, axis, 0, 0)


def exchange_sum(blocks, axis):
    return jnp.sum(lax.all_to_all(blocks, axis, 0, 0).astype(jnp.float32), axis=0)


def beside(blocks, moves):
    blocks, chunks = lax.optimization_barrier((blocks, [chunk for chunk, _, _ in moves]))
    got = [lax.ppermute(c, axis, pairs) for c, (_, axis, pairs) in zip(chunks, moves)]
    return lax.optimization_barrier((lax.all_to_all(blocks, "dp", 0, 0), got))


def with_squares(terms, squares):
    coarse = squares.astype(jnp.bfloat16)
    fine = (squares - coarse.astype(jnp.float32)).astype(jnp.bfloat16)
    return jnp.concatenate([terms, jnp.where(jnp.arange(128) < 64, coarse, fine)], axis=-1)


def normalized(total, width):
    n = total.shape[-1] - 128
    mean = (total[..., n : n + 1] + total[..., n + 64 : n + 65]) / width
    return (total[..., :n] * lax.rsqrt(mean + 1e-06)).astype(jnp.bfloat16)


def add_up(blocks):
    return jnp.sum(blocks.astype(jnp.float32), axis=0)


def from_own(values, place):
    blocks = jnp.split(values, 4, axis=-1)
    near = place % 2 == 1
    far = place >= 2
    paired = [jnp.where(near, blocks[i ^ 1], blocks[i]) for i in range(4)]
    blocks = [jnp.where(far, paired[i ^ 2], paired[i]) for i in range(4)]
    return jnp.concatenate([blocks[0], blocks[2], blocks[1], blocks[3]], axis=-1)


def to_own(values, place):
    blocks = jnp.split(values, 4, axis=-1)
    blocks = [blocks[0], blocks[2], blocks[1], blocks[3]]
    near = place % 2 == 1
    far = place >= 2
    paired = [jnp.where(near, blocks[i ^ 1], blocks[i]) for i in range(4)]
    return jnp.concatenate([jnp.where(far, paired[i ^ 2], paired[i]) for i in range(4)], axis=-1)


def own_rows(full):
    rows = full.shape[0] // lax.axis_size("dp")
    return lax.dynamic_slice_in_dim(full, lax.axis_index("dp") * rows, rows, 0)


def on_device(
    src_embed,
    tgt_embed,
    src_lengths,
    enc_gain,
    enc_project,
    enc_output,
    final_gain,
    dec_gain,
    dec_query,
    dec_memory,
    dec_output,
):
    enc_place = lax.axis_index("enc")
    dec_place = lax.axis_index("dec")
    place = lax.axis_index("dp")
    n_dec = lax.axis_size("dec")
    n_dp = lax.axis_size("dp")
    core = enc_place % 2
    late = enc_place >= 2
    swap = [(0, 1), (1, 0), (2, 3), (3, 2)]
    early, later = (0, 1), (2, 3)
    enc_length = pick_length(src_lengths, dec_place)
    dec_length = pick_length(src_lengths, enc_place)

    src = src_embed[0]
    rows, width = src.shape
    half = rows // 2
    own = half // n_dp
    block = width // n_dec

    shard_memory = dec_memory[0].reshape(block, 2 * HD)

    def far(shard, places):
        pairs = [(e * n_dec + d, (e ^ 2) * n_dec + d) for e in range(4) for d in places]
        return lax.ppermute(shard, ("enc", "dec"), pairs)

    def with_near(mine, axis):
        return jnp.concatenate([mine, lax.ppermute(mine, "enc", swap)], axis=axis)

    def joined(mine, remote, axis):
        return with_near(jnp.concatenate([mine, remote], axis=axis), axis)

    def both(mine):
        other = lax.ppermute(mine, "enc", swap)
        return [jnp.where(core == which, mine, other) for which in range(2)]

    weights_in = both(enc_project[0].reshape(block, 3 * HD))
    weights_out = both(enc_output[0])
    gains = [lax.dynamic_slice_in_dim(g[0], dec_place * block, block) for g in both(enc_gain)]

    mine = lax.dynamic_slice_in_dim(src, core * half, half, 0)
    mine = mine.reshape(half, n_dec, block).transpose(1, 0, 2)
    current = lax.all_to_all(mine, "dec", 0, 0)
    piece = lax.dynamic_slice_in_dim(
        current.reshape(n_dec, n_dp, own, block), place, 1, 1
    ).reshape(n_dec * own, block)
    steps = jnp.arange(half)
    key_places = jnp.concatenate([core * half + steps, (1 - core) * half + steps])
    states = []
    for step in range(4):
        which = step % 2
        wide = current.astype(jnp.float32)
        squares = jnp.sum(wide * wide, axis=-1, keepdims=True)
        scaled = (wide * gains[which]).astype(jnp.bfloat16)
        terms = jnp.einsum(
            "mtc,cn->mtn", scaled, weights_in[which], preferred_element_type=jnp.float32
        ).astype(jnp.bfloat16)
        mixed = normalized(exchange_sum(with_squares(terms, squares), "dec"), width)
        pair = mixed[:, HD:]
        pair = jnp.concatenate([pair, lax.ppermute(pair, "enc", swap)], axis=0)
        attended = attend(mixed[:, :HD], pair[:, :HD], pair[:, HD:], key_places, enc_length)
        everyone = spread(attended, "dec").reshape(n_dec, n_dp, own, HD)
        everyone = everyone.transpose(1, 0, 2, 3).reshape(n_dec * half, HD)
        terms = jnp.dot(everyone, weights_out[which], preferred_element_type=jnp.float32)
        terms = terms.astype(jnp.bfloat16).reshape(n_dp, n_dec * own, block)
        moving = []
        if step == 0:
            terms, shard = lax.optimization_barrier((terms, dec_query[0]))
            moving = [far(shard, early), with_near(shard_memory, 0)]
        elif step == 1:
            terms, shard, far_query = lax.optimization_barrier((terms, dec_output[0], moved[0]))
            dec_weight_memory = moved[1]
        elif step == 2:
            terms, shard = lax.optimization_barrier((terms, dec_query[0]))
            moving = [far(shard, later)]
        else:
            terms, got = lax.optimization_barrier((terms, moved[0]))
            far_query = jnp.where(dec_place < 2, far_query, got)
            dec_weight_query = joined(dec_query[0], far_query, 0)
        terms = lax.all_to_all(terms, "dp", 0, 0)
        if step == 1:
            terms, far_out = lax.optimization_barrier((terms, far(shard, early)))
        summed = add_up(terms)
        piece = (piece.astype(jnp.float32) + summed).astype(jnp.bfloat16)
        states.append(piece)
        if step == 1:
            piece = lax.ppermute(piece, "enc", [(0, 2), (1, 3)])
        if step < 3:
            current = spread(piece, "dp").reshape(n_dp, n_dec, own, block)
            current, moved = lax.optimization_barrier((current, moving))
            current = current.transpose(1, 0, 2, 3).reshape(n_dec, half, block)

    def place_of(n):
        return (
            jnp.arange(n_dp)[:, None, None] * own
            + jnp.arange(2)[None, :, None] * half
            + jnp.arange(own)[None, None, :]
        ).reshape(n)

    blocks = states[3].reshape(2, 2, own, block).transpose(1, 0, 2, 3)
    blocks = jnp.broadcast_to(blocks[None, :, None], (2, 2, n_dec, 2, own, block))
    blocks = lax.all_to_all(blocks.reshape(-1, 2 * own, block), ("enc", "dec"), 0, 0)
    blocks = blocks.reshape(2, 2, 2, 2, 2, own, block)[1]
    blocks = jnp.where(late, blocks[:, 1], blocks[:, 0])
    blocks = jnp.where(core == 0, blocks, blocks[:, ::-1])
    last = blocks.transpose(2, 0, 3, 1, 4).reshape(4 * own, 2 * block)
    last, shard = lax.optimization_barrier((last, dec_output[0]))
    got = far(shard, later)
    last = spread(last, "dp")
    last, got = lax.optimization_barrier((last, got))
    far_out = jnp.where(dec_place < 2, far_out, got)
    dec_weight_out = joined(dec_output[0], far_out, 1)
    gain = jnp.concatenate(
        [
            lax.dynamic_slice_in_dim(final_gain, place * block, block)
            for place in (enc_place, enc_place + 1 - 2 * core)
        ]
    )
    wide = last.astype(jnp.float32)
    squares = jnp.sum(wide * wide, axis=-1, keepdims=True)
    scaled = (wide * gain).astype(jnp.bfloat16)
    terms = jnp.einsum(
        "hrc,cn->hrn", scaled, dec_weight_memory, preferred_element_type=jnp.float32
    )
    sent = with_squares(terms.astype(jnp.bfloat16), squares).reshape(n_dp, 2, 2 * own, -1)
    kept = jnp.where(late, sent[:, 1], sent[:, 0]).reshape(rows, -1)
    given = jnp.where(late, sent[:, 0], sent[:, 1]).reshape(rows, -1)
    total = kept.astype(jnp.float32) + far(given, range(n_dec)).astype(jnp.float32)
    pairs = normalized(total, width)
    keys, values = pairs[:, :HD], pairs[:, HD:]
    memory_places = place_of(rows)

    even = jnp.where(late, states[2], states[0])
    odd = jnp.where(late, states[3], states[1])
    kept = jnp.where(core == 0, even, odd)
    given = lax.ppermute(jnp.where(core == 0, odd, even), "enc", swap)
    halves = jnp.stack([jnp.where(core == 0, kept, given), jnp.where(core == 0, given, kept)])
    halves = halves.reshape(2, n_dec, own, block).transpose(1, 0, 2, 3)
    halves = halves.reshape(n_dec, 2 * own, block)
    moves = []
    for by in range(1, n_dec):
        along = [(i, (i + by) % n_dec) for i in range(n_dec)]
        chunk = lax.dynamic_index_in_dim(halves, (dec_place + by) % n_dec, 0, keepdims=False)
        moves.append((chunk, "dec", along))
    kept = lax.dynamic_index_in_dim(halves, dec_place, 0, keepdims=False)

    def in_order(parts):
        blocks = []
        for source in range(n_dec):
            chosen = parts[0]
            for by in range(1, n_dec):
                chosen = jnp.where((dec_place - by) % n_dec == source, parts[by], chosen)
            blocks.append(chosen)
        return jnp.concatenate(blocks, axis=-1)

    current = from_own(tgt_embed[0], enc_place)
    gain = from_own(dec_gain[0], enc_place)
    piece = own_rows(current)
    dec_piece = piece
    gathered = []
    for step in range(4):
        normed = normalize(current, gain).astype(jnp.bfloat16)
        query = jnp.dot(normed, dec_weight_query, preferred_element_type=jnp.float32)
        attended = attend(query.astype(jnp.bfloat16), keys, values, memory_places, dec_length)
        terms = jnp.dot(attended, dec_weight_out, preferred_element_type=jnp.float32)
        terms = terms.astype(jnp.bfloat16).reshape(n_dp, -1, width)
        if step == 0:
            terms, got = beside(terms, moves)
            enc_piece = in_order([kept] + got)
        elif step == 3:
            enc_state = jnp.where(dec_place == 1, gathered[1], gathered[0])
            enc_state = enc_state.reshape(n_dp, 2, own, width)
            enc_state = enc_state.transpose(1, 0, 2, 3).reshape(rows, width)
            terms, enc_state = lax.optimization_barrier((terms, enc_state))
            terms = lax.all_to_all(terms, "dp", 0, 0)
        else:
            terms = lax.all_to_all(terms, "dp", 0, 0)
        result = (piece.astype(jnp.float32) + add_up(terms)).astype(jnp.bfloat16)
        dec_piece = jnp.where(dec_place == step, result, dec_piece)
        if step < 3:
            piece = lax.ppermute(result, "dec", [(step, step + 1)])
            current = jnp.where(dec_place == step + 1, piece, enc_piece)
            current = spread(current, "dp").reshape(rows, width)
            gathered.append(current)
    dec_state = spread(to_own(dec_piece, enc_place), "dp").reshape(rows, width)
    return (enc_state[None, None], dec_state[None, None])


def solution(mesh):
    placed = (
        P("dec", None, None),
        P("enc", None, None),
        P(),
        P("enc", None),
        P("enc", "dec", None, "dp"),
        P("enc", "dp", "dec"),
        P(),
        P("dec", None),
        P("dec", "enc", "dp"),
        P("dec", "enc", None, "dp"),
        P("dec", "dp", "enc"),
    )
    return jax.shard_map(
        on_device,
        mesh=mesh,
        in_specs=placed,
        out_specs=(P("enc", "dec", None, None), P("dec", "enc", None, None)),
        check_vma=False,
    )
```

```python
import math

import jax
import jax.numpy as jnp
from jax import lax
from jax.sharding import PartitionSpec as P

HD = 256


def normalize(values, gain):
    wide = values.astype(jnp.float32)
    return wide * lax.rsqrt(jnp.mean(wide * wide, axis=-1, keepdims=True) + 1e-06) * gain


def attend(query, keys, values, positions, length):
    scores = lax.dot_general(
        query, keys, (((1,), (1,)), ((), ())), preferred_element_type=jnp.float32
    ) * (1.0 / math.sqrt(HD))
    scores = jnp.where((positions < length)[None, :], scores, -1e30)
    top = jnp.max(scores, axis=-1, keepdims=True)
    weights = jnp.exp(scores - top)
    probs = (weights / jnp.sum(weights, axis=-1, keepdims=True)).astype(jnp.bfloat16)
    return jnp.dot(probs, values, preferred_element_type=jnp.float32).astype(jnp.bfloat16)


def pick_length(table, position):
    return jnp.sum(jnp.where(jnp.arange(table.shape[0]) == position, table, 0))


def spread(block, axis):
    copies = jnp.broadcast_to(block[None], (lax.axis_size(axis),) + block.shape)
    return lax.all_to_all(copies, axis, 0, 0)


def exchange_sum(blocks, axis):
    return jnp.sum(lax.all_to_all(blocks, axis, 0, 0).astype(jnp.float32), axis=0)


def beside(blocks, moves):
    blocks, chunks = lax.optimization_barrier((blocks, [chunk for chunk, _, _ in moves]))
    got = [lax.ppermute(c, axis, pairs) for c, (_, axis, pairs) in zip(chunks, moves)]
    return lax.optimization_barrier((lax.all_to_all(blocks, "dp", 0, 0), got))


def with_squares(terms, squares):
    coarse = squares.astype(jnp.bfloat16)
    fine = (squares - coarse.astype(jnp.float32)).astype(jnp.bfloat16)
    return jnp.concatenate([terms, jnp.where(jnp.arange(128) < 64, coarse, fine)], axis=-1)


def normalized(total, width):
    n = total.shape[-1] - 128
    mean = (total[..., n : n + 1] + total[..., n + 64 : n + 65]) / width
    return (total[..., :n] * lax.rsqrt(mean + 1e-06)).astype(jnp.bfloat16)


def add_up(blocks):
    return jnp.sum(blocks.astype(jnp.float32), axis=0)


def from_own(values, place):
    blocks = jnp.split(values, 4, axis=-1)
    near = place % 2 == 1
    far = place >= 2
    paired = [jnp.where(near, blocks[i ^ 1], blocks[i]) for i in range(4)]
    blocks = [jnp.where(far, paired[i ^ 2], paired[i]) for i in range(4)]
    return jnp.concatenate([blocks[0], blocks[2], blocks[1], blocks[3]], axis=-1)


def to_own(values, place):
    blocks = jnp.split(values, 4, axis=-1)
    blocks = [blocks[0], blocks[2], blocks[1], blocks[3]]
    near = place % 2 == 1
    far = place >= 2
    paired = [jnp.where(near, blocks[i ^ 1], blocks[i]) for i in range(4)]
    return jnp.concatenate([jnp.where(far, paired[i ^ 2], paired[i]) for i in range(4)], axis=-1)


def own_rows(full):
    rows = full.shape[0] // lax.axis_size("dp")
    return lax.dynamic_slice_in_dim(full, lax.axis_index("dp") * rows, rows, 0)


def on_device(
    src_embed,
    tgt_embed,
    src_lengths,
    enc_gain,
    enc_project,
    enc_output,
    final_gain,
    dec_gain,
    dec_query,
    dec_memory,
    dec_output,
):
    enc_place = lax.axis_index("enc")
    dec_place = lax.axis_index("dec")
    place = lax.axis_index("dp")
    n_dec = lax.axis_size("dec")
    n_dp = lax.axis_size("dp")
    core = enc_place % 2
    late = enc_place >= 2
    swap = [(0, 1), (1, 0), (2, 3), (3, 2)]
    early, later = (0, 1), (2, 3)
    enc_length = pick_length(src_lengths, dec_place)
    dec_length = pick_length(src_lengths, enc_place)

    src = src_embed[0]
    rows, width = src.shape
    half = rows // 2
    own = half // n_dp
    block = width // n_dec

    shard_memory = dec_memory[0].reshape(block, 2 * HD)

    def far(shard, places):
        pairs = [(e * n_dec + d, (e ^ 2) * n_dec + d) for e in range(4) for d in places]
        return lax.ppermute(shard, ("enc", "dec"), pairs)

    def with_near(mine, axis):
        return jnp.concatenate([mine, lax.ppermute(mine, "enc", swap)], axis=axis)

    def joined(mine, remote, axis):
        return with_near(jnp.concatenate([mine, remote], axis=axis), axis)

    def both(mine):
        other = lax.ppermute(mine, "enc", swap)
        return [jnp.where(core == which, mine, other) for which in range(2)]

    weights_in = both(enc_project[0].reshape(block, 3 * HD))
    weights_out = both(enc_output[0])
    gains = [lax.dynamic_slice_in_dim(g[0], dec_place * block, block) for g in both(enc_gain)]

    mine = lax.dynamic_slice_in_dim(src, core * half, half, 0)
    mine = mine.reshape(half, n_dec, block).transpose(1, 0, 2)
    current = lax.all_to_all(mine, "dec", 0, 0)
    piece = lax.dynamic_slice_in_dim(
        current.reshape(n_dec, n_dp, own, block), place, 1, 1
    ).reshape(n_dec * own, block)
    steps = jnp.arange(half)
    key_places = jnp.concatenate([core * half + steps, (1 - core) * half + steps])
    states = []
    for step in range(4):
        which = step % 2
        wide = current.astype(jnp.float32)
        squares = jnp.sum(wide * wide, axis=-1, keepdims=True)
        scaled = (wide * gains[which]).astype(jnp.bfloat16)
        terms = jnp.einsum(
            "mtc,cn->mtn", scaled, weights_in[which], preferred_element_type=jnp.float32
        ).astype(jnp.bfloat16)
        mixed = normalized(exchange_sum(with_squares(terms, squares), "dec"), width)
        pair = mixed[:, HD:]
        pair = jnp.concatenate([pair, lax.ppermute(pair, "enc", swap)], axis=0)
        attended = attend(mixed[:, :HD], pair[:, :HD], pair[:, HD:], key_places, enc_length)
        everyone = spread(attended, "dec").reshape(n_dec, n_dp, own, HD)
        everyone = everyone.transpose(1, 0, 2, 3).reshape(n_dec * half, HD)
        terms = jnp.dot(everyone, weights_out[which], preferred_element_type=jnp.float32)
        terms = terms.astype(jnp.bfloat16).reshape(n_dp, n_dec * own, block)
        moving = []
        if step == 0:
            terms, shard = lax.optimization_barrier((terms, dec_query[0]))
            moving = [far(shard, early), with_near(shard_memory, 0)]
        elif step == 1:
            terms, shard, far_query = lax.optimization_barrier((terms, dec_output[0], moved[0]))
            dec_weight_memory = moved[1]
        elif step == 2:
            terms, shard = lax.optimization_barrier((terms, dec_query[0]))
            moving = [far(shard, later)]
        else:
            terms, got = lax.optimization_barrier((terms, moved[0]))
            far_query = jnp.where(dec_place < 2, far_query, got)
            dec_weight_query = joined(dec_query[0], far_query, 0)
        terms = lax.all_to_all(terms, "dp", 0, 0)
        if step == 1:
            terms, far_out = lax.optimization_barrier((terms, far(shard, early)))
        summed = add_up(terms)
        piece = (piece.astype(jnp.float32) + summed).astype(jnp.bfloat16)
        states.append(piece)
        if step == 1:
            piece = lax.ppermute(piece, "enc", [(0, 2), (1, 3)])
        if step < 3:
            current = spread(piece, "dp").reshape(n_dp, n_dec, own, block)
            current, moved = lax.optimization_barrier((current, moving))
            current = current.transpose(1, 0, 2, 3).reshape(n_dec, half, block)

    def place_of(n):
        return (
            jnp.arange(n_dp)[:, None, None] * own
            + jnp.arange(2)[None, :, None] * half
            + jnp.arange(own)[None, None, :]
        ).reshape(n)

    blocks = states[3].reshape(2, 2, own, block).transpose(1, 0, 2, 3)
    blocks = jnp.broadcast_to(blocks[None, :, None], (2, 2, n_dec, 2, own, block))
    blocks = lax.all_to_all(blocks.reshape(-1, 2 * own, block), ("enc", "dec"), 0, 0)
    blocks = blocks.reshape(2, 2, 2, 2, 2, own, block)[1]
    blocks = jnp.where(late, blocks[:, 1], blocks[:, 0])
    blocks = jnp.where(core == 0, blocks, blocks[:, ::-1])
    last = blocks.transpose(2, 0, 3, 1, 4).reshape(4 * own, 2 * block)
    last, shard = lax.optimization_barrier((last, dec_output[0]))
    got = far(shard, later)
    last = spread(last, "dp")
    last, got = lax.optimization_barrier((last, got))
    far_out = jnp.where(dec_place < 2, far_out, got)
    dec_weight_out = joined(dec_output[0], far_out, 1)
    gain = jnp.concatenate(
        [
            lax.dynamic_slice_in_dim(final_gain, place * block, block)
            for place in (enc_place, enc_place + 1 - 2 * core)
        ]
    )
    wide = last.astype(jnp.float32)
    squares = jnp.sum(wide * wide, axis=-1, keepdims=True)
    scaled = (wide * gain).astype(jnp.bfloat16)
    terms = jnp.einsum(
        "hrc,cn->hrn", scaled, dec_weight_memory, preferred_element_type=jnp.float32
    )
    sent = with_squares(terms.astype(jnp.bfloat16), squares).reshape(n_dp, 2, 2 * own, -1)
    kept = jnp.where(late, sent[:, 1], sent[:, 0]).reshape(rows, -1)
    given = jnp.where(late, sent[:, 0], sent[:, 1]).reshape(rows, -1)
    given, dec_weight_out = lax.optimization_barrier((far(given, range(n_dec)), dec_weight_out))
    total = kept.astype(jnp.float32) + given.astype(jnp.float32)
    pairs = normalized(total, width)
    keys, values = pairs[:, :HD], pairs[:, HD:]
    memory_places = place_of(rows)

    even = jnp.where(late, states[2], states[0])
    odd = jnp.where(late, states[3], states[1])
    kept = jnp.where(core == 0, even, odd)
    given = lax.ppermute(jnp.where(core == 0, odd, even), "enc", swap)
    halves = jnp.stack([jnp.where(core == 0, kept, given), jnp.where(core == 0, given, kept)])
    halves = halves.reshape(2, n_dec, own, block).transpose(1, 0, 2, 3)
    halves = halves.reshape(n_dec, 2 * own, block)
    moves = []
    for by in range(1, n_dec):
        along = [(i, (i + by) % n_dec) for i in range(n_dec)]
        chunk = lax.dynamic_index_in_dim(halves, (dec_place + by) % n_dec, 0, keepdims=False)
        moves.append((chunk, "dec", along))
    kept = lax.dynamic_index_in_dim(halves, dec_place, 0, keepdims=False)

    def in_order(parts):
        blocks = []
        for source in range(n_dec):
            chosen = parts[0]
            for by in range(1, n_dec):
                chosen = jnp.where((dec_place - by) % n_dec == source, parts[by], chosen)
            blocks.append(chosen)
        return jnp.concatenate(blocks, axis=-1)

    current = from_own(tgt_embed[0], enc_place)
    gain = from_own(dec_gain[0], enc_place)
    piece = own_rows(current)
    dec_piece = piece
    gathered = []
    for step in range(4):
        normed = normalize(current, gain).astype(jnp.bfloat16)
        query = jnp.dot(normed, dec_weight_query, preferred_element_type=jnp.float32)
        attended = attend(query.astype(jnp.bfloat16), keys, values, memory_places, dec_length)
        terms = jnp.dot(attended, dec_weight_out, preferred_element_type=jnp.float32)
        terms = terms.astype(jnp.bfloat16).reshape(n_dp, -1, width)
        if step == 0:
            terms, got = beside(terms, moves)
            enc_piece = in_order([kept] + got)
        elif step == 3:
            enc_state = jnp.where(dec_place == 1, gathered[1], gathered[0])
            enc_state = enc_state.reshape(n_dp, 2, own, width)
            enc_state = enc_state.transpose(1, 0, 2, 3).reshape(rows, width)
            terms, enc_state = lax.optimization_barrier((terms, enc_state))
            terms = lax.all_to_all(terms, "dp", 0, 0)
        else:
            terms = lax.all_to_all(terms, "dp", 0, 0)
        result = (piece.astype(jnp.float32) + add_up(terms)).astype(jnp.bfloat16)
        dec_piece = jnp.where(dec_place == step, result, dec_piece)
        if step < 3:
            piece = lax.ppermute(result, "dec", [(step, step + 1)])
            current = jnp.where(dec_place == step + 1, piece, enc_piece)
            current = spread(current, "dp").reshape(rows, width)
            gathered.append(current)
    dec_state = spread(to_own(dec_piece, enc_place), "dp").reshape(rows, width)
    return (enc_state[None, None], dec_state[None, None])


def solution(mesh):
    placed = (
        P("dec", None, None),
        P("enc", None, None),
        P(),
        P("enc", None),
        P("enc", "dec", None, "dp"),
        P("enc", "dp", "dec"),
        P(),
        P("dec", None),
        P("dec", "enc", "dp"),
        P("dec", "enc", None, "dp"),
        P("dec", "dp", "enc"),
    )
    return jax.shard_map(
        on_device,
        mesh=mesh,
        in_specs=placed,
        out_specs=(P("enc", "dec", None, None), P("dec", "enc", None, None)),
        check_vma=False,
    )
```
